32 devices in a mesh: expert: 4 (over y, core), dp: 8 (over z, x).
Axes of the slice: x: 2, y: 2, z: 4, core: 2. Of those that a mesh axis runs over, the one named last changes fastest.
Arguments:
- tokens: bfloat16 [4096, 2048], P(('expert', 'dp')), may hold values from -6 to 6
- out_grad: bfloat16 [4096, 2048], P(('expert', 'dp')), may hold values from -6 to 6
- expert_ids: int32 [4096, 1], P(('expert', 'dp')), may hold values from 0 to 15; in each aligned block of 128 rows (0 to 127, 128 to 255, ...) at most 12 rows name the same one
- combine_ints: int32 [4096, 8], P(('expert', 'dp')), may hold values from 1 to 15
- w_gate: bfloat16 [16, 2048, 384], P('expert'), may hold values from -0.125 to 0.125
- w_up: bfloat16 [16, 2048, 384], P('expert'), may hold values from -0.125 to 0.125
- w_down: bfloat16 [16, 384, 2048], P('expert'), may hold values from -0.3125 to 0.3125
Outputs:
- combined: bfloat16 [4096, 2048], P(('expert', 'dp'))
- dinput: bfloat16 [4096, 2048], P(('expert', 'dp'))
- grad_down: float32 [16, 384, 2048], P('expert', None, 'dp')
The draws below stay inside these ranges and needn't reach their ends.
Inputs may be any that keep to these rules, and one draw needn't show every extreme that they name: `expert_ids`: each row names one expert of the window. Among the 128 rows of one device no expert is named more than 12 times, and in every draw some expert is named exactly 12 times by the rows of some device.
All inputs are finite; a program needn't handle non-finite values.
Results may differ from the reference program's by a relative error of at most 0.0057.
Values may be sent and summed in bfloat16 or wider, within the bound.
A program may use at most 64 MiB of HBM per device.

```python
import math
import jax
import jax.numpy as jnp
import numpy as np
from jax import lax

D = 2048
FFW = 384
EXPERTS = 16
TOP = 8
ROUTES = 1
TOK_DEV = 128
CAP = 12
TOKENS = 4096


def set_ends(array, key, low, largest):
    index_at = [jax.random.randint(jax.random.fold_in(key, axis), (), 0, length) for axis, length in enumerate(array.shape)]
    longest = array.shape.index(max(array.shape))
    next_to = index_at[:longest] + [(index_at[longest] + 1) % array.shape[longest]] + index_at[longest + 1:]
    return array.at[tuple(index_at)].set(low).at[tuple(next_to)].set(largest)


def level_of(key, shape, cuts, smallest, high):
    def one(position, parts):
        draws = jax.random.uniform(jax.random.fold_in(jax.random.fold_in(key, 6), position), (parts,), jnp.float32, smallest / len(cuts), high / len(cuts))
        return jnp.repeat(jnp.exp(draws), shape[position] // parts).reshape((-1,) + (1,) * (len(shape) - position - 1))

    factor_of = one(*cuts[0])
    for cut in cuts[1:]:
        factor_of = factor_of * one(*cut)
    return factor_of


def shared_out(rng, own, number, rows, count, top, limit, skew):
    ranking = jax.random.permutation(rng, count)
    crowded, common = portions_of(count, rows * top, limit, skew, True), portions_of(count, rows * top, limit, skew, False)
    places = jnp.arange(count)

    def named(sizes, rotation):
        used = int((sizes > 0).sum())
        fixed = max(1, used // 4)
        passed = fixed + (places - fixed + rotation * (used - fixed)) % max(1, count - fixed)
        return jnp.zeros((count,), jnp.int32).at[ranking[jnp.where(places < fixed, places, passed)]].set(jnp.asarray(sizes, jnp.int32))

    sizes = jnp.where(number % 4 == 0, named(crowded, number // 4), named(common, number - number // 4 - 1))
    mixed = jax.random.permutation(jax.random.fold_in(own, 3), count)
    source_of, receiver = mixed[0:count // 2 * 2:2], mixed[1:count // 2 * 2:2]
    margin = jnp.minimum(sizes[source_of] - 1, limit - sizes[receiver]) // 2
    margin = jnp.where((source_of == ranking[0]) | (receiver == ranking[0]) | (sizes[receiver] == 0), 0, jnp.maximum(margin, 0))
    passed = jax.random.randint(jax.random.fold_in(own, 4), (count // 2,), 0, 1 << 20) % (margin + 1)
    sizes = sizes.at[source_of].add(-passed).at[receiver].add(passed)
    labels = jnp.searchsorted(jnp.cumsum(sizes), jnp.arange(rows * top), side="right").astype(jnp.int32)
    table = labels.reshape(top, rows).T
    table = table[jax.random.permutation(jax.random.fold_in(own, 1), rows)]
    rotation = jax.random.randint(jax.random.fold_in(own, 2), (rows, 1), 0, top)
    return jnp.take_along_axis(table, (jnp.arange(top)[None, :] + rotation) % top, axis=1)


def portions_of(count, total, most, skew, full):
    portions = [(1 << 20) // math.isqrt(rank ** skew) + 1 for rank in range(1, count + 1)]
    largest = most if full else min(most, max(-(-total // count), total * portions[0] // sum(portions)))
    least = 1 if total - largest >= count - 1 else 0
    counts, spare = [largest] + [least] * (count - 1), total - largest - least * (count - 1)
    while spare > 0:
        free = [i for i in range(1, count) if counts[i] < largest] or [i for i in range(1, count) if counts[i] < most]
        pool, left = sum([portions[i] for i in free]), spare
        for i in free:
            extra = min(most - counts[i], max(1, left * portions[i] // pool), spare)
            counts[i] = counts[i] + extra
            spare = spare - extra
    return np.array(counts)


def bell_draw(stream_key, shape, deviation, bound, split=(), kind=jnp.bfloat16):
    values = jax.random.normal(stream_key, shape, jnp.float32) * deviation
    if len(split) > 0:
        values = level_of(stream_key, shape, split, -0.22, 0.18) * values
    return jnp.clip(values, min=-bound, max=bound).astype(kind)


def setup_inputs(seed: int = 0) -> dict:
    key_list = jax.random.split(jax.random.key(seed), 8)
    tokens = bell_draw(key_list[0], (TOKENS, D), 1.0, 6.0, ((0, 32),))
    out_grad = bell_draw(key_list[1], (TOKENS, D), 1.0, 6.0, ((0, 32),))
    expert_ids_keys = jax.random.split(jax.random.fold_in(key_list[2], 1), TOKENS // TOK_DEV)
    expert_ids_turns = jax.random.permutation(jax.random.fold_in(key_list[2], 3), TOKENS // TOK_DEV)
    expert_ids = jax.vmap(lambda own, number: shared_out(jax.random.fold_in(key_list[2], 2), own, number, TOK_DEV, EXPERTS, ROUTES, CAP, 2))(expert_ids_keys, expert_ids_turns).reshape((TOKENS, ROUTES))
    combine_ints = set_ends(jax.random.randint(key_list[3], (TOKENS, TOP), 1, 16), jax.random.fold_in(key_list[3], 1), 1, 15).astype(jnp.int32)
    w_gate = bell_draw(key_list[4], (EXPERTS, D, FFW), D ** -0.5, 0.125, ((0, 4),))
    w_up = bell_draw(key_list[5], (EXPERTS, D, FFW), D ** -0.5, 0.125, ((0, 4),))
    w_down = bell_draw(key_list[6], (EXPERTS, FFW, D), FFW ** -0.5, 0.3125, ((0, 4),))
    return {"tokens": tokens, "out_grad": out_grad, "expert_ids": expert_ids, "combine_ints": combine_ints, "w_gate": w_gate, "w_up": w_up, "w_down": w_down}


def reference(tokens, out_grad, expert_ids, combine_ints, w_gate, w_up, w_down):
    sources = TOKENS // TOK_DEV
    buf_rows = sources * CAP
    flat_ids = expert_ids.reshape(sources, TOK_DEV * ROUTES)
    onehot = (flat_ids[:, :, None] == jnp.arange(EXPERTS, dtype=jnp.int32)[None, None, :]).astype(jnp.int32)
    slot_rank = jnp.sum((jnp.cumsum(onehot, axis=1) - onehot) * onehot, axis=2).reshape(TOKENS, ROUTES)
    block_base = (jnp.arange(TOKENS, dtype=jnp.int32) // TOK_DEV) * CAP
    all_weights = combine_ints.astype(jnp.float32)
    weights = all_weights[:, :ROUTES] / jnp.sum(all_weights, axis=1, keepdims=True)
    grad_full = out_grad.astype(jnp.float32)

    def per_expert(totals, inputs):
        out_sum, grad_sum = totals
        expert, gate_mat, up_mat, down_mat = inputs
        routed = expert_ids == expert
        slot_pos = jnp.where(routed, block_base[:, None] + slot_rank, buf_rows).astype(jnp.int32)
        row_buf = jnp.zeros((buf_rows, D), jnp.bfloat16)
        grad_buf = jnp.zeros((buf_rows, D), jnp.bfloat16)
        for route_k in range(ROUTES):
            row_buf = row_buf.at[slot_pos[:, route_k]].set(tokens, mode="drop")
            scaled = (weights[:, route_k:route_k + 1] * grad_full).astype(jnp.bfloat16)
            grad_buf = grad_buf.at[slot_pos[:, route_k]].set(scaled, mode="drop")
        gate_act = jnp.dot(row_buf, gate_mat, preferred_element_type=jnp.float32)
        up_act = jnp.dot(row_buf, up_mat, preferred_element_type=jnp.float32)
        gate_sig = jax.nn.sigmoid(gate_act)
        gate_silu = gate_act * gate_sig
        hidden = (gate_silu * up_act).astype(jnp.bfloat16)
        result = jnp.dot(hidden, down_mat, preferred_element_type=jnp.float32).astype(jnp.bfloat16)
        dhidden = jnp.dot(grad_buf, down_mat.T, preferred_element_type=jnp.float32)
        grad_gate = (dhidden * up_act * gate_sig * (1.0 + gate_act * (1.0 - gate_sig))).astype(jnp.bfloat16)
        grad_up = (dhidden * gate_silu).astype(jnp.bfloat16)
        slot_grad = (jnp.dot(grad_gate, gate_mat.T, preferred_element_type=jnp.float32)
                     + jnp.dot(grad_up, up_mat.T, preferred_element_type=jnp.float32)).astype(jnp.bfloat16)
        grad_mat = jnp.dot(hidden.T, grad_buf, preferred_element_type=jnp.float32)
        clipped = jnp.minimum(slot_pos, buf_rows - 1)
        for route_k in range(ROUTES):
            picked = routed[:, route_k:route_k + 1]
            out_sum = out_sum + jnp.where(picked, weights[:, route_k:route_k + 1] * result[clipped[:, route_k]].astype(jnp.float32), jnp.float32(0.0))
            grad_sum = grad_sum + jnp.where(picked, slot_grad[clipped[:, route_k]].astype(jnp.float32), jnp.float32(0.0))
        return (out_sum, grad_sum), grad_mat

    start_sums = (jnp.zeros((TOKENS, D), jnp.float32), jnp.zeros((TOKENS, D), jnp.float32))
    (out_sum, grad_sum), grad_down = lax.scan(per_expert, start_sums, (jnp.arange(EXPERTS, dtype=jnp.int32), w_gate, w_up, w_down))
    return out_sum.astype(jnp.bfloat16), grad_sum.astype(jnp.bfloat16), grad_down
```

```python
import jax
import jax.numpy as jnp
from jax import lax
from jax.sharding import PartitionSpec as P

CAP = 12


def body(tokens, out_grad, expert_ids, combine_ints, w_gate, w_up, w_down):
    tok_rows, model_width = tokens.shape
    route_count = expert_ids.shape[1]
    groups = lax.axis_size("expert")
    local_count = w_gate.shape[0]
    experts = groups * local_count
    flat_ids = expert_ids.reshape(-1)
    onehot = (flat_ids[:, None] == jnp.arange(experts, dtype=jnp.int32)[None, :]).astype(jnp.int32)
    slot_rank = jnp.sum((jnp.cumsum(onehot, axis=0) - onehot) * onehot, axis=1)
    slot_index = flat_ids * CAP + slot_rank
    owner_row = jnp.arange(tok_rows * route_count, dtype=jnp.int32) // route_count
    all_weights = combine_ints.astype(jnp.float32)
    weights = (all_weights[:, :route_count] / jnp.sum(all_weights, axis=1, keepdims=True)).reshape(
        -1
    )
    scaled = (weights[:, None] * out_grad[owner_row].astype(jnp.float32)).astype(jnp.bfloat16)
    empty_buf = jnp.zeros((experts * CAP, model_width), jnp.bfloat16)
    send_rows = empty_buf.at[slot_index].set(tokens[owner_row])
    send_grads = empty_buf.at[slot_index].set(scaled)
    recv_rows, recv_grads = (
        lax.all_to_all(send_rows, "expert", split_axis=0, concat_axis=0, tiled=True),
        lax.all_to_all(send_grads, "expert", split_axis=0, concat_axis=0, tiled=True),
    )
    rows_four = recv_rows.reshape(groups, local_count, CAP, model_width)
    grads_four = recv_grads.reshape(groups, local_count, CAP, model_width)
    gate_act = jnp.einsum("slcd,ldf->slcf", rows_four, w_gate, preferred_element_type=jnp.float32)
    up_act = jnp.einsum("slcd,ldf->slcf", rows_four, w_up, preferred_element_type=jnp.float32)
    gate_sig = jax.nn.sigmoid(gate_act)
    gate_silu = gate_act * gate_sig
    hidden = (gate_silu * up_act).astype(jnp.bfloat16)
    result = jnp.einsum(
        "slcf,lfd->slcd", hidden, w_down, preferred_element_type=jnp.float32
    ).astype(jnp.bfloat16)
    returned = lax.all_to_all(
        result.reshape(-1, model_width), "expert", split_axis=0, concat_axis=0, tiled=True
    )
    dhidden = jnp.einsum("slcd,lfd->slcf", grads_four, w_down, preferred_element_type=jnp.float32)
    grad_gate = (dhidden * up_act * gate_sig * (1.0 + gate_act * (1.0 - gate_sig))).astype(
        jnp.bfloat16
    )
    grad_up = (dhidden * gate_silu).astype(jnp.bfloat16)
    slot_grad = (
        jnp.einsum("slcf,ldf->slcd", grad_gate, w_gate, preferred_element_type=jnp.float32)
        + jnp.einsum("slcf,ldf->slcd", grad_up, w_up, preferred_element_type=jnp.float32)
    ).astype(jnp.bfloat16)
    grad_back = lax.all_to_all(
        slot_grad.reshape(-1, model_width), "expert", split_axis=0, concat_axis=0, tiled=True
    )
    parts = lax.axis_size("dp")
    cols = model_width // parts
    hidden_all = lax.all_gather(hidden, "dp", axis=0, tiled=False)
    grad_cols = lax.all_to_all(
        grads_four.reshape(-1, parts, cols).transpose(1, 0, 2), "dp", split_axis=0, concat_axis=0, tiled=True
    ).reshape(parts, groups, local_count, CAP, cols)
    grad_share = jnp.einsum(
        "pslcf,pslcd->lfd", hidden_all, grad_cols, preferred_element_type=jnp.float32
    )
    combined = jnp.sum(
        (weights[:, None] * returned[slot_index].astype(jnp.float32)).reshape(
            tok_rows, route_count, model_width
        ),
        axis=1,
    ).astype(jnp.bfloat16)
    dinput = jnp.sum(
        grad_back[slot_index].astype(jnp.float32).reshape(tok_rows, route_count, model_width),
        axis=1,
    ).astype(jnp.bfloat16)
    return (combined, dinput, grad_share)


def solution(mesh):
    return jax.shard_map(
        body,
        mesh=mesh,
        in_specs=(
            P(("expert", "dp"), None),
            P(("expert", "dp"), None),
            P(("expert", "dp"), None),
            P(("expert", "dp"), None),
            P("expert", None, None),
            P("expert", None, None),
            P("expert", None, None),
        ),
        out_specs=(P(("expert", "dp"), None), P(("expert", "dp"), None), P("expert", None, "dp")),
        check_vma=False,
    )
```

```python
import functools

import jax
import jax.numpy as jnp
import numpy as np
from jax import lax
from jax.experimental import pallas as pl
from jax.experimental.pallas import tpu as pltpu
from jax.sharding import PartitionSpec as P

CAP = 12


def plain_body(tokens, out_grad, expert_ids, combine_ints, w_gate, w_up, w_down):
    tok_rows, model_width = tokens.shape
    route_count = expert_ids.shape[1]
    groups = lax.axis_size("expert")
    local_count = w_gate.shape[0]
    experts = groups * local_count
    flat_ids = expert_ids.reshape(-1)
    onehot = (flat_ids[:, None] == jnp.arange(experts, dtype=jnp.int32)[None, :]).astype(jnp.int32)
    slot_rank = jnp.sum((jnp.cumsum(onehot, axis=0) - onehot) * onehot, axis=1)
    slot_index = flat_ids * CAP + slot_rank
    owner_row = jnp.arange(tok_rows * route_count, dtype=jnp.int32) // route_count
    all_weights = combine_ints.astype(jnp.float32)
    weights = (all_weights[:, :route_count] / jnp.sum(all_weights, axis=1, keepdims=True)).reshape(
        -1
    )
    scaled = (weights[:, None] * out_grad[owner_row].astype(jnp.float32)).astype(jnp.bfloat16)
    empty_buf = jnp.zeros((experts * CAP, model_width), jnp.bfloat16)
    send_rows = empty_buf.at[slot_index].set(tokens[owner_row])
    send_grads = empty_buf.at[slot_index].set(scaled)
    recv_rows, recv_grads = (
        lax.all_to_all(send_rows, "expert", split_axis=0, concat_axis=0, tiled=True),
        lax.all_to_all(send_grads, "expert", split_axis=0, concat_axis=0, tiled=True),
    )
    rows_four = recv_rows.reshape(groups, local_count, CAP, model_width)
    grads_four = recv_grads.reshape(groups, local_count, CAP, model_width)
    gate_act = jnp.einsum("slcd,ldf->slcf", rows_four, w_gate, preferred_element_type=jnp.float32)
    up_act = jnp.einsum("slcd,ldf->slcf", rows_four, w_up, preferred_element_type=jnp.float32)
    gate_sig = jax.nn.sigmoid(gate_act)
    gate_silu = gate_act * gate_sig
    hidden = (gate_silu * up_act).astype(jnp.bfloat16)
    result = jnp.einsum(
        "slcf,lfd->slcd", hidden, w_down, preferred_element_type=jnp.float32
    ).astype(jnp.bfloat16)
    returned = lax.all_to_all(
        result.reshape(-1, model_width), "expert", split_axis=0, concat_axis=0, tiled=True
    )
    dhidden = jnp.einsum("slcd,lfd->slcf", grads_four, w_down, preferred_element_type=jnp.float32)
    grad_gate = (dhidden * up_act * gate_sig * (1.0 + gate_act * (1.0 - gate_sig))).astype(
        jnp.bfloat16
    )
    grad_up = (dhidden * gate_silu).astype(jnp.bfloat16)
    slot_grad = (
        jnp.einsum("slcf,ldf->slcd", grad_gate, w_gate, preferred_element_type=jnp.float32)
        + jnp.einsum("slcf,ldf->slcd", grad_up, w_up, preferred_element_type=jnp.float32)
    ).astype(jnp.bfloat16)
    grad_back = lax.all_to_all(
        slot_grad.reshape(-1, model_width), "expert", split_axis=0, concat_axis=0, tiled=True
    )
    parts = lax.axis_size("dp")
    cols = model_width // parts
    hidden_all = lax.all_gather(hidden, "dp", axis=0, tiled=False)
    grad_cols = lax.all_to_all(
        grads_four.reshape(-1, parts, cols).transpose(1, 0, 2), "dp", split_axis=0, concat_axis=0, tiled=True
    ).reshape(parts, groups, local_count, CAP, cols)
    grad_share = jnp.einsum(
        "pslcf,pslcd->lfd", hidden_all, grad_cols, preferred_element_type=jnp.float32
    )
    combined = jnp.sum(
        (weights[:, None] * returned[slot_index].astype(jnp.float32)).reshape(
            tok_rows, route_count, model_width
        ),
        axis=1,
    ).astype(jnp.bfloat16)
    dinput = jnp.sum(
        grad_back[slot_index].astype(jnp.float32).reshape(tok_rows, route_count, model_width),
        axis=1,
    ).astype(jnp.bfloat16)
    return (combined, dinput, grad_share)


MESH = pl.DeviceIdType.MESH
TN = (((0,), (0,)), ((), ()))
NN = (((1,), (0,)), ((), ()))
NT = (((1,), (1,)), ((), ()))


def mm(a, b, dims):
    return lax.dot_general(a, b, dims, preferred_element_type=jnp.float32)


def kernel(
    groups,
    parts,
    tok_ref,
    og_ref,
    ids_ref,
    ints_ref,
    perm_ref,
    wg_hbm,
    wu_hbm,
    wd_hbm,
    comb_ref,
    din_ref,
    gd_ref,
    wg,
    wu,
    wd,
    x_out,
    g_out,
    x_in,
    g_in,
    rows,
    grads,
    o_out,
    d_out,
    o_in,
    d_in,
    stage,
    gate_s,
    up_s,
    hid,
    cot,
    w_sem,
    exp_send,
    exp_recv,
    dp_send,
    dp_recv,
):
    bf16, f32 = jnp.bfloat16, jnp.float32
    count, width = tok_ref.shape
    local = wg_hbm.shape[0]
    experts = groups * local
    block = local * CAP
    slots = groups * block
    per = groups * CAP
    cols = width // parts
    me_e, me_d = lax.axis_index("expert"), lax.axis_index("dp")

    def w_copy(which, hbm, vmem, l):
        return pltpu.make_async_copy(hbm.at[l], vmem.at[l], w_sem.at[which, l])

    for l in range(local):
        w_copy(0, wg_hbm, wg, l).start()
        w_copy(1, wu_hbm, wu, l).start()
    for l in range(local):
        w_copy(2, wd_hbm, wd, l).start()

    def expert_at(k):
        return {"expert": lax.rem(me_e + k + groups, groups)}

    def dp_at(k):
        return {"dp": lax.rem(me_d + k, parts)}

    barrier = pltpu.get_barrier_semaphore()
    for k in range(1, groups):
        pl.semaphore_signal(barrier, inc=1, device_id=expert_at(k), device_id_type=MESH)
    for k in range(1, parts):
        pl.semaphore_signal(barrier, inc=1, device_id=dp_at(k), device_id_type=MESH)

    ids = ids_ref[...]
    hot = (ids == lax.broadcasted_iota(jnp.int32, (count, experts), 1)).astype(f32)
    earlier = (
        lax.broadcasted_iota(jnp.int32, (count, count), 1)
        < lax.broadcasted_iota(jnp.int32, (count, count), 0)
    ).astype(f32)
    before = mm(earlier.astype(bf16), hot.astype(bf16), NN)
    rank = jnp.sum(before * hot, axis=1, keepdims=True).astype(jnp.int32)
    shifted = ids - me_e * local
    shifted = jnp.where(shifted < 0, shifted + experts, shifted)
    slot = shifted * CAP + rank
    pick = (slot == lax.broadcasted_iota(jnp.int32, (count, slots), 1)).astype(f32).astype(bf16)
    ints = ints_ref[...].astype(f32)
    weight = ints[:, :1] / jnp.sum(ints, axis=1, keepdims=True)

    def to_expert(row, src, dst, k, toward):
        piece = pl.ds(k * block, block)
        return pltpu.make_async_remote_copy(
            src_ref=src.at[piece],
            dst_ref=dst.at[piece],
            send_sem=exp_send.at[row, k],
            recv_sem=exp_recv.at[row, k],
            device_id=expert_at(k if toward else -k),
            device_id_type=MESH,
        )

    ring = sorted(range(1, groups), key=lambda k: abs(2 * k - groups))

    def post(row, src, dst, value, toward):
        src[...] = value.astype(bf16)
        dst[pl.ds(0, block)] = src[pl.ds(0, block)]
        for k in ring:
            to_expert(row, src, dst, k, toward).start()

    def arrived(row, src, dst, toward):
        for k in ring:
            to_expert(row, src, dst, k, toward).wait_recv()

    def to_dp(row, src, dst, k):
        return pltpu.make_async_remote_copy(
            src_ref=src,
            dst_ref=dst.at[k],
            send_sem=dp_send.at[row, k],
            recv_sem=dp_recv.at[row, k],
            device_id=dp_at(k),
            device_id_type=MESH,
        )

    x_value = mm(pick, tok_ref[...], TN)
    pl.semaphore_wait(barrier, groups + parts - 2)
    post(0, x_out, x_in, x_value, True)
    scaled = (weight * og_ref[...].astype(f32)).astype(bf16)
    post(1, g_out, g_in, mm(pick, scaled, TN), True)

    arrived(0, x_out, x_in, True)
    rows[...] = mm(perm_ref[...], x_in[...], NN).astype(bf16)

    def forward(l, carry):
        w_copy(0, wg_hbm, wg, l).wait()
        w_copy(1, wu_hbm, wu, l).wait()
        piece = pl.ds(pl.multiple_of(l * per, per), per)
        x = rows[piece]
        gate = mm(x, wg[l], NN)
        up = mm(x, wu[l], NN)
        gate_s[piece] = gate
        up_s[piece] = up
        hid[0, piece] = (gate * jax.nn.sigmoid(gate) * up).astype(bf16)
        return carry

    lax.fori_loop(0, local, forward, 0)
    for k in range(1, parts):
        to_dp(0, hid.at[0], hid, k).start()

    arrived(1, g_out, g_in, True)
    grads[...] = mm(perm_ref[...], g_in[...], NN).astype(bf16)

    def columns(k):
        return pl.ds(pl.multiple_of(lax.rem(me_d + k, parts) * cols, cols), cols)

    for k in range(1, parts):
        to_dp(1, grads.at[:, columns(k)], cot, k).start()
    cot[0] = grads[:, columns(0)]

    def down(l, carry):
        w_copy(2, wd_hbm, wd, l).wait()
        piece = pl.ds(pl.multiple_of(l * per, per), per)
        stage[piece] = mm(hid[0, piece], wd[l], NN).astype(bf16)
        return carry

    lax.fori_loop(0, local, down, 0)
    post(2, o_out, o_in, mm(perm_ref[...], stage[...], TN), False)

    def backward(l, carry):
        piece = pl.ds(pl.multiple_of(l * per, per), per)
        dh = mm(grads[piece], wd[l], NT)
        gate, up = gate_s[piece], up_s[piece]
        sig = jax.nn.sigmoid(gate)
        d_gate = (dh * up * sig * (1.0 + gate * (1.0 - sig))).astype(bf16)
        d_up = (dh * (gate * sig)).astype(bf16)
        stage[piece] = (mm(d_gate, wg[l], NT) + mm(d_up, wu[l], NT)).astype(bf16)
        return carry

    lax.fori_loop(0, local, backward, 0)
    post(3, d_out, d_in, mm(perm_ref[...], stage[...], TN), False)

    arrived(2, o_out, o_in, False)
    comb_ref[...] = (weight * mm(pick, o_in[...], NN)).astype(bf16)

    for k in range(1, parts):
        to_dp(0, hid.at[0], hid, k).wait_recv()
    for k in range(1, parts):
        to_dp(1, grads.at[:, columns(k)], cot, k).wait_recv()

    def down_grad(l, carry):
        piece = pl.ds(pl.multiple_of(l * per, per), per)
        h = hid[:, piece].reshape(parts * per, hid.shape[2])
        c = cot[:, piece].reshape(parts * per, cols)
        gd_ref[l] = mm(h, c, TN)
        return carry

    lax.fori_loop(0, local, down_grad, 0)

    arrived(3, d_out, d_in, False)
    din_ref[...] = mm(pick, d_in[...], NN).astype(bf16)

    for k in ring:
        to_expert(0, x_out, x_in, k, True).wait_send()
        to_expert(1, g_out, g_in, k, True).wait_send()
        to_expert(2, o_out, o_in, k, False).wait_send()
        to_expert(3, d_out, d_in, k, False).wait_send()
    for k in range(1, parts):
        to_dp(0, hid.at[0], hid, k).wait_send()
        to_dp(1, grads.at[:, columns(k)], cot, k).wait_send()


def body(tokens, out_grad, expert_ids, combine_ints, w_gate, w_up, w_down):
    count, width = tokens.shape
    groups, parts = lax.axis_size("expert"), lax.axis_size("dp")
    local, _, inner = w_gate.shape
    block, per, cols = local * CAP, groups * CAP, width // parts
    if expert_ids.shape[1] != 1 or block % 16 or per % 16 or cols % 128:
        return plain_body(tokens, out_grad, expert_ids, combine_ints, w_gate, w_up, w_down)
    slots = groups * block
    order = np.arange(slots).reshape(groups, local, CAP).transpose(1, 0, 2).reshape(-1)
    perm = jnp.asarray(np.eye(slots, dtype=np.float32)[order], jnp.bfloat16)
    bf16, f32 = jnp.bfloat16, jnp.float32
    vmem = pl.BlockSpec(memory_space=pltpu.VMEM)
    hbm = pl.BlockSpec(memory_space=pl.ANY)
    wide = pltpu.VMEM((slots, width), bf16)
    return pl.pallas_call(
        functools.partial(kernel, groups, parts),
        out_shape=(
            jax.ShapeDtypeStruct((count, width), bf16),
            jax.ShapeDtypeStruct((count, width), bf16),
            jax.ShapeDtypeStruct((local, inner, cols), f32),
        ),
        in_specs=[vmem] * 5 + [hbm] * 3,
        out_specs=(vmem, vmem, vmem),
        scratch_shapes=[
            pltpu.VMEM(w_gate.shape, bf16),
            pltpu.VMEM(w_up.shape, bf16),
            pltpu.VMEM(w_down.shape, bf16),
        ]
        + [wide] * 11
        + [
            pltpu.VMEM((slots, inner), f32),
            pltpu.VMEM((slots, inner), f32),
            pltpu.VMEM((parts, slots, inner), bf16),
            pltpu.VMEM((parts, slots, cols), bf16),
            pltpu.SemaphoreType.DMA((3, local)),
            pltpu.SemaphoreType.DMA((4, groups)),
            pltpu.SemaphoreType.DMA((4, groups)),
            pltpu.SemaphoreType.DMA((2, parts)),
            pltpu.SemaphoreType.DMA((2, parts)),
        ],
        compiler_params=pltpu.CompilerParams(
            collective_id=0, has_side_effects=True, vmem_limit_bytes=58 * 2**20
        ),
    )(tokens, out_grad, expert_ids, combine_ints, perm, w_gate, w_up, w_down)


def solution(mesh):
    return jax.shard_map(
        body,
        mesh=mesh,
        in_specs=(
            P(("expert", "dp"), None),
            P(("expert", "dp"), None),
            P(("expert", "dp"), None),
            P(("expert", "dp"), None),
            P("expert", None, None),
            P("expert", None, None),
            P("expert", None, None),
        ),
        out_specs=(P(("expert", "dp"), None), P(("expert", "dp"), None), P("expert", None, "dp")),
        check_vma=False,
    )
```

```python
import functools

import jax
import jax.numpy as jnp
import numpy as np
from jax import lax
from jax.experimental import pallas as pl
from jax.experimental.pallas import tpu as pltpu
from jax.sharding import PartitionSpec as P

CAP = 12


def plain_body(tokens, out_grad, expert_ids, combine_ints, w_gate, w_up, w_down):
    tok_rows, model_width = tokens.shape
    route_count = expert_ids.shape[1]
    groups = lax.axis_size("expert")
    local_count = w_gate.shape[0]
    experts = groups * local_count
    flat_ids = expert_ids.reshape(-1)
    onehot = (flat_ids[:, None] == jnp.arange(experts, dtype=jnp.int32)[None, :]).astype(jnp.int32)
    slot_rank = jnp.sum((jnp.cumsum(onehot, axis=0) - onehot) * onehot, axis=1)
    slot_index = flat_ids * CAP + slot_rank
    owner_row = jnp.arange(tok_rows * route_count, dtype=jnp.int32) // route_count
    all_weights = combine_ints.astype(jnp.float32)
    weights = (all_weights[:, :route_count] / jnp.sum(all_weights, axis=1, keepdims=True)).reshape(
        -1
    )
    scaled = (weights[:, None] * out_grad[owner_row].astype(jnp.float32)).astype(jnp.bfloat16)
    empty_buf = jnp.zeros((experts * CAP, model_width), jnp.bfloat16)
    send_rows = empty_buf.at[slot_index].set(tokens[owner_row])
    send_grads = empty_buf.at[slot_index].set(scaled)
    recv_rows, recv_grads = (
        lax.all_to_all(send_rows, "expert", split_axis=0, concat_axis=0, tiled=True),
        lax.all_to_all(send_grads, "expert", split_axis=0, concat_axis=0, tiled=True),
    )
    rows_four = recv_rows.reshape(groups, local_count, CAP, model_width)
    grads_four = recv_grads.reshape(groups, local_count, CAP, model_width)
    gate_act = jnp.einsum("slcd,ldf->slcf", rows_four, w_gate, preferred_element_type=jnp.float32)
    up_act = jnp.einsum("slcd,ldf->slcf", rows_four, w_up, preferred_element_type=jnp.float32)
    gate_sig = jax.nn.sigmoid(gate_act)
    gate_silu = gate_act * gate_sig
    hidden = (gate_silu * up_act).astype(jnp.bfloat16)
    result = jnp.einsum(
        "slcf,lfd->slcd", hidden, w_down, preferred_element_type=jnp.float32
    ).astype(jnp.bfloat16)
    returned = lax.all_to_all(
        result.reshape(-1, model_width), "expert", split_axis=0, concat_axis=0, tiled=True
    )
    dhidden = jnp.einsum("slcd,lfd->slcf", grads_four, w_down, preferred_element_type=jnp.float32)
    grad_gate = (dhidden * up_act * gate_sig * (1.0 + gate_act * (1.0 - gate_sig))).astype(
        jnp.bfloat16
    )
    grad_up = (dhidden * gate_silu).astype(jnp.bfloat16)
    slot_grad = (
        jnp.einsum("slcf,ldf->slcd", grad_gate, w_gate, preferred_element_type=jnp.float32)
        + jnp.einsum("slcf,ldf->slcd", grad_up, w_up, preferred_element_type=jnp.float32)
    ).astype(jnp.bfloat16)
    grad_back = lax.all_to_all(
        slot_grad.reshape(-1, model_width), "expert", split_axis=0, concat_axis=0, tiled=True
    )
    parts = lax.axis_size("dp")
    cols = model_width // parts
    hidden_all = lax.all_gather(hidden, "dp", axis=0, tiled=False)
    grad_cols = lax.all_to_all(
        grads_four.reshape(-1, parts, cols).transpose(1, 0, 2), "dp", split_axis=0, concat_axis=0, tiled=True
    ).reshape(parts, groups, local_count, CAP, cols)
    grad_share = jnp.einsum(
        "pslcf,pslcd->lfd", hidden_all, grad_cols, preferred_element_type=jnp.float32
    )
    combined = jnp.sum(
        (weights[:, None] * returned[slot_index].astype(jnp.float32)).reshape(
            tok_rows, route_count, model_width
        ),
        axis=1,
    ).astype(jnp.bfloat16)
    dinput = jnp.sum(
        grad_back[slot_index].astype(jnp.float32).reshape(tok_rows, route_count, model_width),
        axis=1,
    ).astype(jnp.bfloat16)
    return (combined, dinput, grad_share)


MESH = pl.DeviceIdType.MESH
TN = (((0,), (0,)), ((), ()))
NN = (((1,), (0,)), ((), ()))
NT = (((1,), (1,)), ((), ()))


def mm(a, b, dims):
    return lax.dot_general(a, b, dims, preferred_element_type=jnp.float32)


def kernel(
    groups,
    parts,
    tok_ref,
    og_ref,
    routing_ref,
    base_ref,
    perm_ref,
    wg_hbm,
    wu_hbm,
    wd_hbm,
    comb_ref,
    din_ref,
    gd_ref,
    wg,
    wu,
    wd,
    x_out,
    g_out,
    x_in,
    g_in,
    rows,
    grads,
    o_out,
    d_out,
    o_in,
    d_in,
    stage,
    gate_s,
    up_s,
    hid,
    cot,
    cot_rows,
    w_sem,
    exp_send,
    exp_recv,
    hid_send,
    hid_recv,
    cot_send,
    cot_recv,
):
    bf16, f32 = jnp.bfloat16, jnp.float32
    count, width = tok_ref.shape
    local = wg_hbm.shape[0]
    experts = groups * local
    block = local * CAP
    slots = groups * block
    per = groups * CAP
    cols = width // parts
    me_e, me_d = lax.axis_index("expert"), lax.axis_index("dp")

    def w_copy(which, hbm, vmem, l):
        return pltpu.make_async_copy(hbm.at[l], vmem.at[l], w_sem.at[which, l])

    for l in range(local):
        w_copy(0, wg_hbm, wg, l).start()
        w_copy(1, wu_hbm, wu, l).start()
    for l in range(local):
        w_copy(2, wd_hbm, wd, l).start()

    def partner(i):
        return i + 1 - 2 * lax.rem(i, 2)

    def ahead(i, slot, n):
        there = lax.rem(i + slot - slot % 2, n)
        return partner(there) if slot % 2 else there

    def behind(i, slot, n):
        return lax.rem((partner(i) if slot % 2 else i) - (slot - slot % 2) + n, n)

    barrier = pltpu.get_barrier_semaphore()
    for k in range(1, groups):
        pl.semaphore_signal(barrier, inc=1, device_id={"expert": ahead(me_e, k, groups)}, device_id_type=MESH)
    for k in range(1, parts):
        pl.semaphore_signal(barrier, inc=1, device_id={"dp": ahead(me_d, k, parts)}, device_id_type=MESH)

    routing = routing_ref[...]
    side = lax.rem(me_e, 2)
    shifted = routing[:, :1] - (me_e - side) * local
    shifted = jnp.where(shifted < 0, shifted + experts, shifted)
    hot = (shifted == lax.broadcasted_iota(jnp.int32, (count, experts), 1)).astype(f32)
    earlier = (
        lax.broadcasted_iota(jnp.int32, (count, count), 1)
        < lax.broadcasted_iota(jnp.int32, (count, count), 0)
    ).astype(f32)
    before = mm(earlier.astype(bf16), hot.astype(bf16), NN)
    odd = side.astype(f32)
    base = base_ref[0:1] * (1.0 - odd) + base_ref[1:2] * odd
    slot = jnp.sum((before + base) * hot, axis=1, keepdims=True).astype(jnp.int32)
    pick = (slot == lax.broadcasted_iota(jnp.int32, (count, slots), 1)).astype(f32).astype(bf16)
    ints = routing[:, 1:].astype(f32)
    weight = ints[:, :1] / jnp.sum(ints, axis=1, keepdims=True)

    def to_expert(row, src, dst, k, toward):
        piece = pl.ds(k * block, block)
        return pltpu.make_async_remote_copy(
            src_ref=src.at[piece],
            dst_ref=dst.at[piece],
            send_sem=exp_send.at[row, k],
            recv_sem=exp_recv.at[row, k],
            device_id={"expert": (ahead if toward else behind)(me_e, k, groups)},
            device_id_type=MESH,
        )

    ring = [*range(2, groups), 1]

    def post(row, src, dst, value, toward):
        src[...] = value.astype(bf16)
        dst[pl.ds(0, block)] = src[pl.ds(0, block)]
        for k in ring:
            to_expert(row, src, dst, k, toward).start()

    def arrived(row, src, dst, toward):
        for k in ring:
            to_expert(row, src, dst, k, toward).wait_recv()

    def hid_copy(l, slot):
        piece = pl.ds(pl.multiple_of(l * per, per), per)
        relay = slot % 2
        return pltpu.make_async_remote_copy(
            src_ref=hid.at[slot - relay if relay else 0, piece],
            dst_ref=hid.at[slot, piece],
            send_sem=hid_send.at[l, slot],
            recv_sem=hid_recv.at[l, slot],
            device_id={"dp": partner(me_d) if relay else ahead(me_d, slot, parts)},
            device_id_type=MESH,
        )

    def columns(slot):
        return pl.ds(pl.multiple_of(ahead(me_d, slot, parts) * cols, cols), cols)

    def cot_copy(j, slot):
        piece = pl.ds(j * block, block)
        return pltpu.make_async_remote_copy(
            src_ref=g_in.at[piece, columns(slot)],
            dst_ref=cot.at[slot, piece],
            send_sem=cot_send.at[j, slot],
            recv_sem=cot_recv.at[j, slot],
            device_id={"dp": ahead(me_d, slot, parts)},
            device_id_type=MESH,
        )

    def send_columns(j):
        for slot in range(1, parts):
            cot_copy(j, slot).start()

    x_value = mm(pick, tok_ref[...], TN)
    pl.semaphore_wait(barrier, groups + parts - 2)
    post(0, x_out, x_in, x_value, True)
    scaled = (weight * og_ref[...].astype(f32)).astype(bf16)
    post(1, g_out, g_in, mm(pick, scaled, TN), True)
    send_columns(0)
    to_expert(1, g_out, g_in, 1, True).wait_recv()
    send_columns(1)

    arrived(0, x_out, x_in, True)
    rows[...] = mm(perm_ref[...], x_in[...], NN).astype(bf16)

    def forward(l, carry):
        w_copy(0, wg_hbm, wg, l).wait()
        w_copy(1, wu_hbm, wu, l).wait()
        piece = pl.ds(pl.multiple_of(l * per, per), per)
        x = rows[piece]
        gate = mm(x, wg[l], NN)
        up = mm(x, wu[l], NN)
        gate_s[piece] = gate
        up_s[piece] = up
        hid[0, piece] = (gate * jax.nn.sigmoid(gate) * up).astype(bf16)
        for slot in (*range(2, parts, 2), 1):
            hid_copy(l, slot).start()
        return carry

    lax.fori_loop(0, local, forward, 0)
    def down(l, carry):
        w_copy(2, wd_hbm, wd, l).wait()
        piece = pl.ds(pl.multiple_of(l * per, per), per)
        stage[piece] = mm(hid[0, piece], wd[l], NN).astype(bf16)
        return carry

    lax.fori_loop(0, local, down, 0)
    post(2, o_out, o_in, mm(perm_ref[...], stage[...], TN), False)

    for j in range(2, groups):
        to_expert(1, g_out, g_in, j, True).wait_recv()
        send_columns(j)
    grads[...] = mm(perm_ref[...], g_in[...], NN).astype(bf16)
    cot[0] = g_in[:, columns(0)]

    def backward(l, carry):
        piece = pl.ds(pl.multiple_of(l * per, per), per)
        dh = mm(grads[piece], wd[l], NT)
        gate, up = gate_s[piece], up_s[piece]
        sig = jax.nn.sigmoid(gate)
        d_gate = (dh * up * sig * (1.0 + gate * (1.0 - sig))).astype(bf16)
        d_up = (dh * (gate * sig)).astype(bf16)
        stage[piece] = (mm(d_gate, wg[l], NT) + mm(d_up, wu[l], NT)).astype(bf16)
        return carry

    lax.fori_loop(0, local, backward, 0)
    post(3, d_out, d_in, mm(perm_ref[...], stage[...], TN), False)

    def relay(l, carry):
        for slot in range(2, parts, 2):
            hid_copy(l, slot).wait_recv()
            hid_copy(l, slot + 1).start()
        return carry

    lax.fori_loop(0, local, relay, 0)

    arrived(2, o_out, o_in, False)
    comb_ref[...] = (weight * mm(pick, o_in[...], NN)).astype(bf16)

    for j in range(groups):
        for slot in range(1, parts):
            cot_copy(j, slot).wait_recv()

    def regroup(p, carry):
        cot_rows[p] = mm(perm_ref[...], cot[p], NN).astype(bf16)
        return carry

    lax.fori_loop(0, parts, regroup, 0)

    def down_grad(l, carry):
        for slot in range(1, parts, 2):
            hid_copy(l, slot).wait_recv()
        piece = pl.ds(pl.multiple_of(l * per, per), per)
        h = hid[:, piece].reshape(parts * per, hid.shape[2])
        c = cot_rows[:, piece].reshape(parts * per, cols)
        gd_ref[l] = mm(h, c, TN)
        return carry

    lax.fori_loop(0, local, down_grad, 0)

    arrived(3, d_out, d_in, False)
    din_ref[...] = mm(pick, d_in[...], NN).astype(bf16)

    for k in ring:
        to_expert(0, x_out, x_in, k, True).wait_send()
        to_expert(1, g_out, g_in, k, True).wait_send()
        to_expert(2, o_out, o_in, k, False).wait_send()
        to_expert(3, d_out, d_in, k, False).wait_send()

    def sent(l, carry):
        for slot in range(1, parts):
            hid_copy(l, slot).wait_send()
        return carry

    lax.fori_loop(0, local, sent, 0)
    for j in range(groups):
        for slot in range(1, parts):
            cot_copy(j, slot).wait_send()


def body(tokens, out_grad, expert_ids, combine_ints, w_gate, w_up, w_down):
    count, width = tokens.shape
    groups, parts = lax.axis_size("expert"), lax.axis_size("dp")
    local, _, inner = w_gate.shape
    block, per, cols = local * CAP, groups * CAP, width // parts
    if expert_ids.shape[1] != 1 or groups % 2 or parts % 2 or block % 16 or per % 16 or cols % 128:
        return plain_body(tokens, out_grad, expert_ids, combine_ints, w_gate, w_up, w_down)
    slots = groups * block
    order = np.arange(slots).reshape(groups, local, CAP).transpose(1, 0, 2).reshape(-1)
    perm = jnp.asarray(np.eye(slots, dtype=np.float32)[order], jnp.bfloat16)
    unit = np.arange(groups * local)
    swapped = (unit // local ^ 1) * local + unit % local
    base = jnp.asarray(np.stack([unit, swapped]) * CAP, jnp.float32)
    routing = jnp.concatenate([expert_ids, combine_ints], axis=1)
    bf16, f32 = jnp.bfloat16, jnp.float32
    vmem = pl.BlockSpec(memory_space=pltpu.VMEM)
    hbm = pl.BlockSpec(memory_space=pl.ANY)
    wide = pltpu.VMEM((slots, width), bf16)
    return pl.pallas_call(
        functools.partial(kernel, groups, parts),
        out_shape=(
            jax.ShapeDtypeStruct((count, width), bf16),
            jax.ShapeDtypeStruct((count, width), bf16),
            jax.ShapeDtypeStruct((local, inner, cols), f32),
        ),
        in_specs=[vmem] * 5 + [hbm] * 3,
        out_specs=(vmem, vmem, vmem),
        scratch_shapes=[
            pltpu.VMEM(w_gate.shape, bf16),
            pltpu.VMEM(w_up.shape, bf16),
            pltpu.VMEM(w_down.shape, bf16),
        ]
        + [wide] * 11
        + [
            pltpu.VMEM((slots, inner), f32),
            pltpu.VMEM((slots, inner), f32),
            pltpu.VMEM((parts, slots, inner), bf16),
            pltpu.VMEM((parts, slots, cols), bf16),
            pltpu.VMEM((parts, slots, cols), bf16),
            pltpu.SemaphoreType.DMA((3, local)),
            pltpu.SemaphoreType.DMA((4, groups)),
            pltpu.SemaphoreType.DMA((4, groups)),
            pltpu.SemaphoreType.DMA((local, parts)),
            pltpu.SemaphoreType.DMA((local, parts)),
            pltpu.SemaphoreType.DMA((groups, parts)),
            pltpu.SemaphoreType.DMA((groups, parts)),
        ],
        compiler_params=pltpu.CompilerParams(
            collective_id=0, has_side_effects=True, vmem_limit_bytes=58 * 2**20
        ),
    )(tokens, out_grad, routing, base, perm, w_gate, w_up, w_down)


def solution(mesh):
    return jax.shard_map(
        body,
        mesh=mesh,
        in_specs=(
            P(("expert", "dp"), None),
            P(("expert", "dp"), None),
            P(("expert", "dp"), None),
            P(("expert", "dp"), None),
            P("expert", None, None),
            P("expert", None, None),
            P("expert", None, None),
        ),
        out_specs=(P(("expert", "dp"), None), P(("expert", "dp"), None), P("expert", None, "dp")),
        check_vma=False,
    )
```

```python
import functools

import jax
import jax.numpy as jnp
import numpy as np
from jax import lax
from jax.experimental import pallas as pl
from jax.experimental.pallas import tpu as pltpu
from jax.sharding import PartitionSpec as P

CAP = 12


def plain_body(tokens, out_grad, expert_ids, combine_ints, w_gate, w_up, w_down):
    tok_rows, model_width = tokens.shape
    route_count = expert_ids.shape[1]
    groups = lax.axis_size("expert")
    local_count = w_gate.shape[0]
    experts = groups * local_count
    flat_ids = expert_ids.reshape(-1)
    onehot = (flat_ids[:, None] == jnp.arange(experts, dtype=jnp.int32)[None, :]).astype(jnp.int32)
    slot_rank = jnp.sum((jnp.cumsum(onehot, axis=0) - onehot) * onehot, axis=1)
    slot_index = flat_ids * CAP + slot_rank
    owner_row = jnp.arange(tok_rows * route_count, dtype=jnp.int32) // route_count
    all_weights = combine_ints.astype(jnp.float32)
    weights = (all_weights[:, :route_count] / jnp.sum(all_weights, axis=1, keepdims=True)).reshape(
        -1
    )
    scaled = (weights[:, None] * out_grad[owner_row].astype(jnp.float32)).astype(jnp.bfloat16)
    empty_buf = jnp.zeros((experts * CAP, model_width), jnp.bfloat16)
    send_rows = empty_buf.at[slot_index].set(tokens[owner_row])
    send_grads = empty_buf.at[slot_index].set(scaled)
    recv_rows, recv_grads = (
        lax.all_to_all(send_rows, "expert", split_axis=0, concat_axis=0, tiled=True),
        lax.all_to_all(send_grads, "expert", split_axis=0, concat_axis=0, tiled=True),
    )
    rows_four = recv_rows.reshape(groups, local_count, CAP, model_width)
    grads_four = recv_grads.reshape(groups, local_count, CAP, model_width)
    gate_act = jnp.einsum("slcd,ldf->slcf", rows_four, w_gate, preferred_element_type=jnp.float32)
    up_act = jnp.einsum("slcd,ldf->slcf", rows_four, w_up, preferred_element_type=jnp.float32)
    gate_sig = jax.nn.sigmoid(gate_act)
    gate_silu = gate_act * gate_sig
    hidden = (gate_silu * up_act).astype(jnp.bfloat16)
    result = jnp.einsum(
        "slcf,lfd->slcd", hidden, w_down, preferred_element_type=jnp.float32
    ).astype(jnp.bfloat16)
    returned = lax.all_to_all(
        result.reshape(-1, model_width), "expert", split_axis=0, concat_axis=0, tiled=True
    )
    dhidden = jnp.einsum("slcd,lfd->slcf", grads_four, w_down, preferred_element_type=jnp.float32)
    grad_gate = (dhidden * up_act * gate_sig * (1.0 + gate_act * (1.0 - gate_sig))).astype(
        jnp.bfloat16
    )
    grad_up = (dhidden * gate_silu).astype(jnp.bfloat16)
    slot_grad = (
        jnp.einsum("slcf,ldf->slcd", grad_gate, w_gate, preferred_element_type=jnp.float32)
        + jnp.einsum("slcf,ldf->slcd", grad_up, w_up, preferred_element_type=jnp.float32)
    ).astype(jnp.bfloat16)
    grad_back = lax.all_to_all(
        slot_grad.reshape(-1, model_width), "expert", split_axis=0, concat_axis=0, tiled=True
    )
    parts = lax.axis_size("dp")
    cols = model_width // parts
    hidden_all = lax.all_gather(hidden, "dp", axis=0, tiled=False)
    grad_cols = lax.all_to_all(
        grads_four.reshape(-1, parts, cols).transpose(1, 0, 2), "dp", split_axis=0, concat_axis=0, tiled=True
    ).reshape(parts, groups, local_count, CAP, cols)
    grad_share = jnp.einsum(
        "pslcf,pslcd->lfd", hidden_all, grad_cols, preferred_element_type=jnp.float32
    )
    combined = jnp.sum(
        (weights[:, None] * returned[slot_index].astype(jnp.float32)).reshape(
            tok_rows, route_count, model_width
        ),
        axis=1,
    ).astype(jnp.bfloat16)
    dinput = jnp.sum(
        grad_back[slot_index].astype(jnp.float32).reshape(tok_rows, route_count, model_width),
        axis=1,
    ).astype(jnp.bfloat16)
    return (combined, dinput, grad_share)


MESH = pl.DeviceIdType.MESH
TN = (((0,), (0,)), ((), ()))
NN = (((1,), (0,)), ((), ()))
NT = (((1,), (1,)), ((), ()))


def mm(a, b, dims):
    return lax.dot_general(a, b, dims, preferred_element_type=jnp.float32)


def kernel(
    groups,
    parts,
    tok_hbm,
    og_hbm,
    routing_ref,
    base_ref,
    perm_ref,
    wg_hbm,
    wu_hbm,
    wd_hbm,
    comb_hbm,
    din_hbm,
    gd_hbm,
    tok_ref,
    og_ref,
    comb_ref,
    din_ref,
    gd_ref,
    wg,
    wu,
    wd,
    x_out,
    g_out,
    x_in,
    g_in,
    rows,
    grads,
    o_out,
    d_out,
    o_in,
    d_in,
    stage,
    gate_s,
    up_s,
    hid,
    cot,
    cot_rows,
    w_sem,
    io_sem,
    exp_send,
    exp_recv,
    hid_send,
    hid_recv,
    cot_send,
    cot_recv,
):
    bf16, f32 = jnp.bfloat16, jnp.float32
    count, width = tok_hbm.shape
    local = wg_hbm.shape[0]
    experts = groups * local
    block = local * CAP
    slots = groups * block
    per = groups * CAP
    cols = width // parts
    me_e, me_d = lax.axis_index("expert"), lax.axis_index("dp")

    def w_copy(which, hbm, vmem, l):
        return pltpu.make_async_copy(hbm.at[l], vmem.at[l], w_sem.at[which, l])

    tok_copy = pltpu.make_async_copy(tok_hbm, tok_ref, io_sem.at[0])
    og_copy = pltpu.make_async_copy(og_hbm, og_ref, io_sem.at[1])
    tok_copy.start()
    og_copy.start()

    def partner(i):
        return i + 1 - 2 * lax.rem(i, 2)

    def ahead(i, slot, n):
        there = lax.rem(i + slot - slot % 2, n)
        return partner(there) if slot % 2 else there

    def behind(i, slot, n):
        return lax.rem((partner(i) if slot % 2 else i) - (slot - slot % 2) + n, n)

    barrier = pltpu.get_barrier_semaphore()
    for k in range(1, groups):
        pl.semaphore_signal(barrier, inc=1, device_id={"expert": ahead(me_e, k, groups)}, device_id_type=MESH)
    for k in range(1, parts):
        pl.semaphore_signal(barrier, inc=1, device_id={"dp": ahead(me_d, k, parts)}, device_id_type=MESH)

    for l in range(local):
        w_copy(0, wg_hbm, wg, l).start()
        w_copy(1, wu_hbm, wu, l).start()
    for l in range(local):
        w_copy(2, wd_hbm, wd, l).start()

    routing = routing_ref[...]
    side = lax.rem(me_e, 2)
    shifted = routing[:, :1] - (me_e - side) * local
    shifted = jnp.where(shifted < 0, shifted + experts, shifted)
    hot = (shifted == lax.broadcasted_iota(jnp.int32, (count, experts), 1)).astype(f32)
    earlier = (
        lax.broadcasted_iota(jnp.int32, (count, count), 1)
        < lax.broadcasted_iota(jnp.int32, (count, count), 0)
    ).astype(f32)
    before = mm(earlier.astype(bf16), hot.astype(bf16), NN)
    odd = side.astype(f32)
    base = base_ref[0:1] * (1.0 - odd) + base_ref[1:2] * odd
    slot = jnp.sum((before + base) * hot, axis=1, keepdims=True).astype(jnp.int32)
    pick = (slot == lax.broadcasted_iota(jnp.int32, (count, slots), 1)).astype(f32).astype(bf16)
    ints = routing[:, 1:].astype(f32)
    weight = ints[:, :1] / jnp.sum(ints, axis=1, keepdims=True)

    def to_expert(row, src, dst, k, toward):
        piece = pl.ds(k * block, block)
        return pltpu.make_async_remote_copy(
            src_ref=src.at[piece],
            dst_ref=dst.at[piece],
            send_sem=exp_send.at[row, k],
            recv_sem=exp_recv.at[row, k],
            device_id={"expert": (ahead if toward else behind)(me_e, k, groups)},
            device_id_type=MESH,
        )

    ring = [*range(2, groups), 1]

    def post(row, src, dst, value, toward):
        src[...] = value.astype(bf16)
        dst[pl.ds(0, block)] = src[pl.ds(0, block)]
        for k in ring:
            to_expert(row, src, dst, k, toward).start()

    def arrived(row, src, dst, toward):
        for k in ring:
            to_expert(row, src, dst, k, toward).wait_recv()

    def hid_copy(l, slot):
        piece = pl.ds(pl.multiple_of(l * per, per), per)
        relay = slot % 2
        return pltpu.make_async_remote_copy(
            src_ref=hid.at[slot - relay if relay else 0, piece],
            dst_ref=hid.at[slot, piece],
            send_sem=hid_send.at[l, slot],
            recv_sem=hid_recv.at[l, slot],
            device_id={"dp": partner(me_d) if relay else ahead(me_d, slot, parts)},
            device_id_type=MESH,
        )

    def columns(slot):
        return pl.ds(pl.multiple_of(ahead(me_d, slot, parts) * cols, cols), cols)

    def cot_copy(j, slot):
        piece = pl.ds(j * block, block)
        return pltpu.make_async_remote_copy(
            src_ref=g_in.at[piece, columns(slot)],
            dst_ref=cot.at[slot, piece],
            send_sem=cot_send.at[j, slot],
            recv_sem=cot_recv.at[j, slot],
            device_id={"dp": ahead(me_d, slot, parts)},
            device_id_type=MESH,
        )

    def send_columns(j):
        for slot in range(1, parts):
            cot_copy(j, slot).start()

    tok_copy.wait()
    x_value = mm(pick, tok_ref[...], TN)
    pl.semaphore_wait(barrier, groups + parts - 2)
    post(0, x_out, x_in, x_value, True)
    og_copy.wait()
    scaled = (weight * og_ref[...].astype(f32)).astype(bf16)
    post(1, g_out, g_in, mm(pick, scaled, TN), True)
    send_columns(0)
    to_expert(1, g_out, g_in, 1, True).wait_recv()
    send_columns(1)

    arrived(0, x_out, x_in, True)
    rows[...] = mm(perm_ref[...], x_in[...], NN).astype(bf16)

    def forward(l, carry):
        w_copy(0, wg_hbm, wg, l).wait()
        w_copy(1, wu_hbm, wu, l).wait()
        piece = pl.ds(pl.multiple_of(l * per, per), per)
        x = rows[piece]
        gate = mm(x, wg[l], NN)
        up = mm(x, wu[l], NN)
        gate_s[piece] = gate
        up_s[piece] = up
        hid[0, piece] = (gate * jax.nn.sigmoid(gate) * up).astype(bf16)
        for slot in (*range(2, parts, 2), 1):
            hid_copy(l, slot).start()
        return carry

    lax.fori_loop(0, local, forward, 0)
    def down(l, carry):
        w_copy(2, wd_hbm, wd, l).wait()
        piece = pl.ds(pl.multiple_of(l * per, per), per)
        stage[piece] = mm(hid[0, piece], wd[l], NN).astype(bf16)
        return carry

    lax.fori_loop(0, local, down, 0)
    post(2, o_out, o_in, mm(perm_ref[...], stage[...], TN), False)

    for j in range(2, groups):
        to_expert(1, g_out, g_in, j, True).wait_recv()
        send_columns(j)
    grads[...] = mm(perm_ref[...], g_in[...], NN).astype(bf16)
    cot[0] = g_in[:, columns(0)]

    def backward(l, carry):
        piece = pl.ds(pl.multiple_of(l * per, per), per)
        dh = mm(grads[piece], wd[l], NT)
        gate, up = gate_s[piece], up_s[piece]
        sig = jax.nn.sigmoid(gate)
        d_gate = (dh * up * sig * (1.0 + gate * (1.0 - sig))).astype(bf16)
        d_up = (dh * (gate * sig)).astype(bf16)
        stage[piece] = (mm(d_gate, wg[l], NT) + mm(d_up, wu[l], NT)).astype(bf16)
        return carry

    lax.fori_loop(0, local, backward, 0)
    post(3, d_out, d_in, mm(perm_ref[...], stage[...], TN), False)

    def relay(l, carry):
        for slot in range(2, parts, 2):
            hid_copy(l, slot).wait_recv()
            hid_copy(l, slot + 1).start()
        return carry

    lax.fori_loop(0, local, relay, 0)

    arrived(2, o_out, o_in, False)
    comb_ref[...] = (weight * mm(pick, o_in[...], NN)).astype(bf16)
    comb_copy = pltpu.make_async_copy(comb_ref, comb_hbm, io_sem.at[2])
    comb_copy.start()

    for j in range(groups):
        for slot in range(1, parts):
            cot_copy(j, slot).wait_recv()

    def regroup(p, carry):
        cot_rows[p] = mm(perm_ref[...], cot[p], NN).astype(bf16)
        return carry

    lax.fori_loop(0, parts, regroup, 0)

    def gd_copy(l):
        return pltpu.make_async_copy(gd_ref.at[l], gd_hbm.at[l], w_sem.at[0, l])

    def down_grad(l, carry):
        for slot in range(1, parts, 2):
            hid_copy(l, slot).wait_recv()
        piece = pl.ds(pl.multiple_of(l * per, per), per)
        h = hid[:, piece].reshape(parts * per, hid.shape[2])
        c = cot_rows[:, piece].reshape(parts * per, cols)
        gd_ref[l] = mm(h, c, TN)
        gd_copy(l).start()
        return carry

    lax.fori_loop(0, local, down_grad, 0)

    arrived(3, d_out, d_in, False)
    din_ref[...] = mm(pick, d_in[...], NN).astype(bf16)
    din_copy = pltpu.make_async_copy(din_ref, din_hbm, io_sem.at[3])
    din_copy.start()

    for k in ring:
        to_expert(0, x_out, x_in, k, True).wait_send()
        to_expert(1, g_out, g_in, k, True).wait_send()
        to_expert(2, o_out, o_in, k, False).wait_send()
        to_expert(3, d_out, d_in, k, False).wait_send()

    def sent(l, carry):
        for slot in range(1, parts):
            hid_copy(l, slot).wait_send()
        return carry

    lax.fori_loop(0, local, sent, 0)
    for j in range(groups):
        for slot in range(1, parts):
            cot_copy(j, slot).wait_send()
    comb_copy.wait()
    din_copy.wait()
    for l in range(local):
        gd_copy(l).wait()


def settle(count, *refs):
    sources, results, held = refs[:count], refs[count : 2 * count], refs[2 * count : 3 * count]
    sem = refs[-1]

    def copy(i, j, stage):
        rows = sources[i].shape[0] // 4
        piece = pl.ds(j * rows, rows)
        chain = sources[i].at[piece], held[i].at[piece], results[i].at[piece]
        return pltpu.make_async_copy(chain[stage], chain[stage + 1], sem.at[stage, i, j])

    pieces = [(i, j) for i in range(count) for j in range(4)]
    for i, j in pieces:
        copy(i, j, 0).start()
    for i, j in pieces:
        copy(i, j, 0).wait()
        copy(i, j, 1).start()
    for i, j in pieces:
        copy(i, j, 1).wait()


def body(tokens, out_grad, expert_ids, combine_ints, w_gate, w_up, w_down):
    count, width = tokens.shape
    groups, parts = lax.axis_size("expert"), lax.axis_size("dp")
    local, _, inner = w_gate.shape
    block, per, cols = local * CAP, groups * CAP, width // parts
    if expert_ids.shape[1] != 1 or groups % 2 or parts % 2 or block % 16 or per % 16 or count % 64 or local % 4 or cols % 128:
        return plain_body(tokens, out_grad, expert_ids, combine_ints, w_gate, w_up, w_down)
    slots = groups * block
    order = np.arange(slots).reshape(groups, local, CAP).transpose(1, 0, 2).reshape(-1)
    perm = jnp.asarray(np.eye(slots, dtype=np.float32)[order], jnp.bfloat16)
    unit = np.arange(groups * local)
    swapped = (unit // local ^ 1) * local + unit % local
    base = jnp.asarray(np.stack([unit, swapped]) * CAP, jnp.float32)
    routing = jnp.concatenate([expert_ids, combine_ints], axis=1)
    bf16, f32 = jnp.bfloat16, jnp.float32
    vmem = pl.BlockSpec(memory_space=pltpu.VMEM)
    hbm = pl.BlockSpec(memory_space=pl.ANY)
    wide = pltpu.VMEM((slots, width), bf16)
    found = pl.pallas_call(
        functools.partial(kernel, groups, parts),
        out_shape=(
            jax.ShapeDtypeStruct((count, width), bf16),
            jax.ShapeDtypeStruct((count, width), bf16),
            jax.ShapeDtypeStruct((local, inner, cols), f32),
        ),
        in_specs=[hbm] * 2 + [vmem] * 3 + [hbm] * 3,
        out_specs=(hbm, hbm, hbm),
        scratch_shapes=[
            pltpu.VMEM((count, width), bf16),
            pltpu.VMEM((count, width), bf16),
            pltpu.VMEM((count, width), bf16),
            pltpu.VMEM((count, width), bf16),
            pltpu.VMEM((local, inner, cols), f32),
            pltpu.VMEM(w_gate.shape, bf16),
            pltpu.VMEM(w_up.shape, bf16),
            pltpu.VMEM(w_down.shape, bf16),
        ]
        + [wide] * 11
        + [
            pltpu.VMEM((slots, inner), f32),
            pltpu.VMEM((slots, inner), f32),
            pltpu.VMEM((parts, slots, inner), bf16),
            pltpu.VMEM((parts, slots, cols), bf16),
            pltpu.VMEM((parts, slots, cols), bf16),
            pltpu.SemaphoreType.DMA((3, local)),
            pltpu.SemaphoreType.DMA((4,)),
            pltpu.SemaphoreType.DMA((4, groups)),
            pltpu.SemaphoreType.DMA((4, groups)),
            pltpu.SemaphoreType.DMA((local, parts)),
            pltpu.SemaphoreType.DMA((local, parts)),
            pltpu.SemaphoreType.DMA((groups, parts)),
            pltpu.SemaphoreType.DMA((groups, parts)),
        ],
        compiler_params=pltpu.CompilerParams(
            collective_id=0, has_side_effects=True, vmem_limit_bytes=58 * 2**20
        ),
    )(tokens, out_grad, routing, base, perm, w_gate, w_up, w_down)
    return pl.pallas_call(
        functools.partial(settle, len(found)),
        out_shape=tuple(jax.ShapeDtypeStruct(a.shape, a.dtype) for a in found),
        in_specs=[hbm] * len(found),
        out_specs=(hbm,) * len(found),
        scratch_shapes=[pltpu.VMEM(a.shape, a.dtype) for a in found]
        + [pltpu.SemaphoreType.DMA((2, len(found), 4))],
        compiler_params=pltpu.CompilerParams(vmem_limit_bytes=58 * 2**20),
    )(*found)


def solution(mesh):
    return jax.shard_map(
        body,
        mesh=mesh,
        in_specs=(
            P(("expert", "dp"), None),
            P(("expert", "dp"), None),
            P(("expert", "dp"), None),
            P(("expert", "dp"), None),
            P("expert", None, None),
            P("expert", None, None),
            P("expert", None, None),
        ),
        out_specs=(P(("expert", "dp"), None), P(("expert", "dp"), None), P("expert", None, "dp")),
        check_vma=False,
    )
```
